512 devices in a mesh: fsdp: 16 (over x, y_lo, core), seq: 32 (over z, y_hi).
Axes of the slice: x: 4, y: 8 (y_hi: 4, y_lo: 2; y = y_hi * 2 + y_lo), z: 8, core: 2. Of those that a mesh axis runs over, the one named last changes fastest.
Arguments:
- conv_input: bfloat16 [16, 4096, 5120], P('fsdp', 'seq'), may hold values from -6 to 6
- gate_input: bfloat16 [16, 4096, 4096], P('fsdp', 'seq'), may hold values from -6 to 6
- step_input: bfloat16 [16, 4096, 64], P('fsdp', 'seq'), may hold values from -3 to 3
- conv_weight: float32 [4, 5120], P(None, 'fsdp'), may hold values from -3 to 3
- conv_bias: float32 [5120], P('fsdp'), may hold values from -3 to 3
- decay_log: float32 [64], P('fsdp'), may hold values from -2.1 to 1.7
- step_bias: float32 [64], P('fsdp'), may hold values from -13 to -3.7
- skip_weight: float32 [64], P('fsdp'), may hold values from 0.5 to 2
- norm_gain: float32 [4096], P('fsdp'), may hold values from 0.5 to 1.5
Outputs:
- mixer_out: bfloat16 [16, 4096, 4096], P('fsdp', 'seq')
The draws below stay inside these ranges and needn't reach their ends.
All inputs are finite; a program needn't handle non-finite values.
Results may differ from the reference program's by a relative error of at most 0.0045.
Values may be sent and summed in bfloat16 or wider, within the bound.
A program may use at most 192 MiB of HBM per device.

```python
import jax
import jax.numpy as jnp
from jax import lax

HEADS = 64
HEAD_DIM = 64
STATE = 128
GROUPS = 4
KERNEL = 4
BLOCK = 128
PROMPTS = 16
SEQLEN = 4096
INNER = 4096
CONV_DIM = 5120


def head_rates(key, lowest, highest):
    unit_draw = jax.random.uniform(key, (HEADS,), jnp.float32)
    rate_values = jnp.exp(jnp.log(lowest) + unit_draw * (jnp.log(highest) - jnp.log(lowest)))
    jitter_factor = jnp.exp(jax.random.uniform(jax.random.fold_in(key, 7), (HEADS,), jnp.float32, -0.7, 0.7))
    dt_level = 0.4 * jnp.maximum(rate_values, 1.0 / SEQLEN) / jitter_factor
    return (rate_values, dt_level)


def draw_decay_log(key, part):
    rate_values, dt_level = head_rates(key, 0.1 / SEQLEN, 0.03)
    return jnp.log(rate_values / dt_level)


def draw_step_bias(key, part):
    rate_values, dt_level = head_rates(key, 0.1 / SEQLEN, 0.03)
    return jnp.log(jnp.expm1(dt_level))


def level_of(rng, shape, cuts, smallest, top_value):
    loudness = 1.0
    for position, blocks in cuts:
        draws = jax.random.uniform(jax.random.fold_in(jax.random.fold_in(rng, 6), position), (blocks,), jnp.float32, smallest / len(cuts), top_value / len(cuts))
        loudness = loudness * jnp.repeat(jnp.exp(draws), shape[position] // blocks).reshape((-1,) + (1,) * (len(shape) - 1 - position))
    return loudness


def normal_values(rng, dims, scale, most, cuts=(), kind=jnp.bfloat16):
    result = scale * jax.random.normal(rng, dims, jnp.float32)
    if cuts:
        result = result * level_of(rng, dims, cuts, -0.22, 0.18)
    return jnp.clip(result, -most, most).astype(kind)


def setup_inputs(seed: int = 0) -> dict:
    arg_keys = jax.random.split(jax.random.key(seed), 10)
    return {
        "conv_input": normal_values(arg_keys[0], (PROMPTS, SEQLEN, CONV_DIM), 1.0, 6.0, ((0, 16), (1, 32))),
        "gate_input": normal_values(arg_keys[1], (PROMPTS, SEQLEN, INNER), 1.0, 6.0, ((0, 16), (1, 32))),
        "step_input": normal_values(arg_keys[2], (PROMPTS, SEQLEN, HEADS), 0.5, 3.0, ((0, 16), (1, 32))),
        "conv_weight": normal_values(arg_keys[3], (KERNEL, CONV_DIM), KERNEL ** -0.5, 3.0, ((1, 16),), jnp.float32),
        "conv_bias": normal_values(arg_keys[4], (CONV_DIM,), 0.5, 3.0, ((0, 16),), jnp.float32),
        "decay_log": draw_decay_log(jax.random.fold_in(arg_keys[9], 71), 0),
        "step_bias": draw_step_bias(jax.random.fold_in(arg_keys[9], 71), 0),
        "skip_weight": jnp.clip(0.5 + 1.5 * jax.random.uniform(arg_keys[7], (HEADS,), jnp.float32) ** level_of(arg_keys[7], (HEADS,), ((0, 16),), -0.2, 0.2), 0.5, 2.0),
        "norm_gain": jnp.clip(1.0 + 0.1 * jax.random.normal(arg_keys[8], (INNER,), jnp.float32), 0.5, 1.5),
    }


HIGH = lax.Precision.HIGHEST
EPS = 1e-05

def mix_inputs(padded_rows, conv_weight, conv_bias, step_rows, step_bias, decay_log):
    length = padded_rows.shape[0] - (KERNEL - 1)
    summed = conv_bias[None, :] + jnp.zeros((length, CONV_DIM), jnp.float32)
    for offset in range(KERNEL):
        summed = summed + conv_weight[offset][None, :] * padded_rows[offset:offset + length]
    activated = jax.nn.silu(summed)
    input_flat = activated[:, :INNER]
    key_flat = activated[:, INNER:INNER + GROUPS * STATE]
    query_flat = activated[:, INNER + GROUPS * STATE:]
    dt_step = jax.nn.softplus(step_rows.astype(jnp.float32) + step_bias[None, :])
    return (input_flat, key_flat, query_flat, dt_step, -jnp.exp(decay_log))

def run_block(memory, in_block, key_block, query_block, step_block, rate_coef):
    length = in_block.shape[2]
    per_group = HEADS // GROUPS
    cumul = jnp.cumsum(step_block * rate_coef[:, None], axis=1)
    positions = jnp.arange(length)
    causal = (positions[:, None] >= positions[None, :])[None, :, :]
    spread = jnp.where(causal, cumul[:, :, None] - cumul[:, None, :], 0.0)
    decays = jnp.where(causal, jnp.exp(spread), 0.0)
    scores = jnp.einsum('gtn,gsn->gts', query_block, key_block, precision=HIGH)
    weights = decays.reshape(GROUPS, per_group, length, length) * scores[:, None, :, :] * step_block.reshape(GROUPS, per_group, 1, length)
    input_groups = in_block.reshape(GROUPS, per_group, HEAD_DIM, length)
    inside = jnp.einsum('gkts,gkps->gkpt', weights, input_groups, precision=HIGH).reshape(HEADS, HEAD_DIM, length)
    carried = jnp.einsum('gtn,gmn->gmt', query_block, memory.reshape(GROUPS, per_group * HEAD_DIM, STATE), precision=HIGH)
    inside = inside + jnp.exp(cumul)[:, None, :] * carried.reshape(HEADS, HEAD_DIM, length)
    remaining = (jnp.exp(cumul[:, -1:] - cumul) * step_block).reshape(GROUPS, per_group, 1, length)
    update = jnp.einsum('gkps,gsn->gkpn', input_groups * remaining, key_block, precision=HIGH)
    new_memory = update.reshape(HEADS, HEAD_DIM, STATE) + jnp.exp(cumul[:, -1])[:, None, None] * memory
    return (new_memory, inside)

def stack_blocks(input_flat, key_flat, query_flat, dt_step):
    count = input_flat.shape[0] // BLOCK
    return (input_flat.reshape(count, BLOCK, HEADS, HEAD_DIM).transpose(0, 2, 3, 1), key_flat.reshape(count, BLOCK, GROUPS, STATE).transpose(0, 2, 1, 3), query_flat.reshape(count, BLOCK, GROUPS, STATE).transpose(0, 2, 1, 3), dt_step.reshape(count, BLOCK, HEADS).transpose(0, 2, 1))

def gated_norm(values, gate_rows, norm_gain):
    length = values.shape[0]
    gated_rows = values * jax.nn.silu(gate_rows.astype(jnp.float32))
    grouped = gated_rows.reshape(length, GROUPS, INNER // GROUPS)
    inverse_rms = lax.rsqrt(lax.optimization_barrier(jnp.mean(grouped * grouped, axis=2, keepdims=True)) + EPS)
    return ((grouped * inverse_rms).reshape(length, INNER) * norm_gain[None, :]).astype(jnp.bfloat16)

def one_prompt(conv_rows, gate_rows, step_rows, conv_weight, conv_bias, decay_log, step_bias, skip_weight, norm_gain):
    padded_rows = jnp.concatenate([jnp.zeros((KERNEL - 1, CONV_DIM), jnp.float32), conv_rows.astype(jnp.float32)], 0)
    input_flat, key_flat, query_flat, dt_step, rate_coef = mix_inputs(padded_rows, conv_weight, conv_bias, step_rows, step_bias, decay_log)

    def advance(memory, pieces):
        return run_block(memory, pieces[0], pieces[1], pieces[2], pieces[3], rate_coef)
    stacked = stack_blocks(input_flat, key_flat, query_flat, dt_step)
    _, outputs = lax.scan(advance, jnp.zeros((HEADS, HEAD_DIM, STATE), jnp.float32), stacked)
    values = outputs.transpose(0, 3, 1, 2).reshape(SEQLEN, INNER) + jnp.repeat(skip_weight, HEAD_DIM)[None, :] * input_flat
    return gated_norm(values, gate_rows, norm_gain)

def reference(conv_input, gate_input, step_input, conv_weight, conv_bias, decay_log, step_bias, skip_weight, norm_gain):

    def per_prompt(prompt_rows):
        return one_prompt(prompt_rows[0], prompt_rows[1], prompt_rows[2], conv_weight, conv_bias, decay_log, step_bias, skip_weight, norm_gain)
    return lax.map(per_prompt, (conv_input, gate_input, step_input))
```

```python
import functools

import jax
import jax.numpy as jnp
from jax import lax
from jax.experimental import pallas as pl
from jax.experimental.pallas import tpu as pltpu
from jax.sharding import PartitionSpec as P

HEADS = 64
GROUPS = 4
KERNEL = 4
INNER = 4096
CONV_DIM = 5120
EPS = 1e-05
ROWS = 128
LANES = 128
TILES = INNER // LANES
PER_GROUP = TILES // GROUPS
LOG2E = 1.4426950408889634
MESH = pl.DeviceIdType.MESH
F32 = jnp.float32
BF16 = jnp.bfloat16


def dot(a, b):
    return jnp.dot(a, b, preferred_element_type=F32)


def silu(v):
    half = 0.5 * v
    return half + half * jnp.tanh(half)


def three_parts(v):
    top = v.astype(BF16).astype(F32)
    rest = v - top
    middle = rest.astype(BF16).astype(F32)
    return top, middle, rest - middle


def remote(src, dst, send, recv, device):
    return pltpu.make_async_remote_copy(
        src_ref=src, dst_ref=dst, send_sem=send, recv_sem=recv,
        device_id=device, device_id_type=MESH,
    )


def kernel(
    ranks, shards,
    conv_hbm, gate_hbm, step_hbm, weight_ref, bias_ref, decay_ref, step_bias_ref, skip_ref, gain_ref,
    out_hbm,
    conv_v, gate_v, step_v, tail_v, halo_pack, halo_send, halo_recv, halo,
    par_send, par, wfull, gfull,
    wide, cparts, logdt, keyt, query, scores,
    xs, vals, expc, gates, square, out_v,
    local_send, local_recv, decay_send, decay_recv, state_send, state_recv,
    load_sem, out_sem, halo_sem, par_sem, loc_sem, dec_sem, st_send_sem, st_recv_sem,
):
    me = lax.axis_index("seq")
    shard = lax.axis_index("fsdp")

    def load(src, dst, slot):
        return pltpu.make_async_copy(src, dst, load_sem.at[slot])

    tail_load = load(conv_hbm.at[0, pl.ds(ROWS - 16, 16)], tail_v, 0)
    step_load = load(step_hbm.at[0], step_v, 1)
    conv_load = load(conv_hbm.at[0], conv_v, 2)
    gate_load = load(gate_hbm.at[0], gate_v, 3)
    tail_load.start()
    step_load.start()
    conv_load.start()
    gate_load.start()

    barrier = pltpu.get_barrier_semaphore()

    def greet_rank(k, c):
        pl.semaphore_signal(barrier, inc=1, device_id={"seq": lax.rem(me + k, ranks)}, device_id_type=MESH)
        return c

    def greet_shard(k, c):
        pl.semaphore_signal(barrier, inc=1, device_id={"fsdp": lax.rem(shard + k, shards)}, device_id_type=MESH)
        return c

    lax.fori_loop(1, shards, greet_shard, 0)
    lax.fori_loop(1, ranks, greet_rank, 0)

    width = CONV_DIM // shards
    heads = HEADS // shards
    par_send[...] = jnp.zeros_like(par_send)
    odd = lax.rem(shard, 2)

    @pl.when(odd == 0)
    def _():
        par_send[0:4, 0:width] = weight_ref[...]
        par_send[4:5, 0:width] = bias_ref[...].reshape(1, width)

    @pl.when(odd == 1)
    def _():
        par_send[0:4, 64 : 64 + width] = weight_ref[...]
        par_send[4:5, 64 : 64 + width] = bias_ref[...].reshape(1, width)

    par_send[5:6, 0:256] = gain_ref[...].reshape(1, 256)
    lane = lax.broadcasted_iota(jnp.int32, (1, LANES), 1)
    for place, ref in enumerate((decay_ref, step_bias_ref, skip_ref)):
        row = jnp.zeros((1, LANES), F32)
        for h in range(heads):
            row = jnp.where(lane == shard * heads + h, ref[h], row)
            row = jnp.where(lane == HEADS + shard * heads + h, ref[h], row)
        par_send[6:7, place * LANES : (place + 1) * LANES] = row

    tail_load.wait()
    halo_pack[15:16, :] = jnp.zeros((1, 1024), F32)
    tail = tail_v[...].astype(F32)
    for r in range(KERNEL - 1):
        for c in range(CONV_DIM // 1024):
            halo_pack[r * 5 + c : r * 5 + c + 1, :] = tail[13 + r : 14 + r, c * 1024 : (c + 1) * 1024]
    halo_send[...] = halo_pack[...].astype(BF16)

    pl.semaphore_wait(barrier, ranks + shards - 2)

    halo_copy = remote(halo_send, halo_recv, halo_sem.at[0], halo_sem.at[1], {"seq": lax.rem(me + 1, ranks)})
    halo_copy.start()

    def send_par(k, c):
        remote(par_send, par.at[shard], par_sem.at[0], par_sem.at[1],
               {"fsdp": lax.rem(shard + k, shards)}).start()
        return c

    lax.fori_loop(1, shards, send_par, 0)
    par[shard] = par_send[...]

    gate_load.wait()

    def gate_tile(o, c):
        at = pl.ds(pl.multiple_of(o * LANES, LANES), LANES)
        gates[o] = silu(gate_v[:, at].astype(F32)).astype(gates.dtype)
        return c

    lax.fori_loop(0, TILES, gate_tile, 0)
    conv_load.wait()
    step_load.wait()

    several = par.at[pl.ds(0, shards - 1)]
    pltpu.make_async_copy(several, several, par_sem.at[1]).wait()
    for j in range(shards // 2):
        left, right = par[2 * j], par[2 * j + 1]
        at = 5 * j * LANES
        wfull[:, at : at + 256] = left[:, 0:256]
        wfull[:, at + 256 : at + 384] = left[:, 256:384] + right[:, 0:128]
        wfull[:, at + 384 : at + 640] = right[:, 128:384]
    small = jnp.zeros((1, 3 * LANES), F32)
    for i in range(shards):
        gfull[:, i * 256 : (i + 1) * 256] = par[i, 5:6, 0:256]
        small = small + par[i, 6:7, :]
    decay_row, bias_row, skip_row = (small[:, i * LANES : (i + 1) * LANES] for i in range(3))

    halo_copy.wait()
    before = jnp.where(me == 0, 0.0, halo_recv[...].astype(F32))
    for r in range(KERNEL - 1):
        for c in range(CONV_DIM // 1024):
            halo[5 + r : 6 + r, c * 1024 : (c + 1) * 1024] = before[r * 5 + c : r * 5 + c + 1, :]

    def convolved(at):
        rows = jnp.concatenate([halo[:, at], conv_v[:, at].astype(F32)], axis=0)
        taps = wfull[:, at]
        total = taps[4:5] + taps[3:4] * rows[8:]
        for back in range(1, KERNEL):
            total = total + taps[3 - back : 4 - back] * pltpu.roll(rows, back, 0)[8:]
        return silu(total)

    step = step_v[...].astype(F32)
    step = jnp.concatenate([step, step], axis=0).T
    dt = jax.nn.softplus(step + bias_row)
    after = lax.broadcasted_iota(jnp.int32, (ROWS, ROWS), 0)
    ahead = lax.broadcasted_iota(jnp.int32, (ROWS, ROWS), 1)
    causal = after >= ahead
    lower = jnp.where(causal, 1.0, 0.0)
    rate2 = -jnp.exp(decay_row) * LOG2E
    cumul = jnp.dot(lower, dt * rate2, precision=lax.Precision.HIGHEST, preferred_element_type=F32)
    low_half = lax.broadcasted_iota(jnp.int32, (ROWS, LANES), 1) < HEADS

    def spread_parts(v):
        top, middle, low = three_parts(v)
        first = jnp.where(low_half[: v.shape[0]], top, middle)
        return first.astype(BF16), jnp.where(low_half[: v.shape[0]], low, 0.0).astype(BF16)

    cparts[:, 0:LANES], cparts[:, LANES:] = spread_parts(cumul)
    logdt[...] = jnp.log2(dt).T - cumul.T
    wide[0:ROWS, 0:LANES], wide[0:ROWS, LANES:] = spread_parts(dt * jnp.exp2(cumul[ROWS - 1 : ROWS] - cumul))
    wide[ROWS : 2 * ROWS, 0:LANES], wide[ROWS : 2 * ROWS, LANES:] = spread_parts(jnp.exp2(cumul))
    skip16 = jnp.broadcast_to(skip_row, (16, LANES))
    wide[2 * ROWS :, 0:LANES], wide[2 * ROWS :, LANES:] = spread_parts(skip16)

    for g in range(GROUPS):
        keys = convolved(slice(INNER + g * LANES, INNER + (g + 1) * LANES))
        keyt[g] = keys.T.astype(BF16)
        asked = convolved(slice(INNER + (GROUPS + g) * LANES, INNER + (GROUPS + g + 1) * LANES))
        query[g] = asked.astype(BF16)
        scores[g] = jnp.where(causal, dot(query[g], keyt[g]), 0.0)

    pick_row = lax.rem(lax.broadcasted_iota(jnp.int32, (2 * LANES, LANES), 0), HEADS)
    pick_half = lax.broadcasted_iota(jnp.int32, (2 * LANES, LANES), 1) // HEADS

    def local_state(o, state_ref, decay_out):
        at = pl.ds(pl.multiple_of(o * LANES, LANES), LANES)
        x = convolved(at)
        pick = jnp.where(pick_row == pick_half + 2 * o, 1.0, 0.0).astype(BF16)
        spread = dot(wide[...], pick)
        expc[o] = spread[ROWS : 2 * ROWS]
        xs[o] = x.astype(BF16)
        vals[o] = x * spread[2 * ROWS : 2 * ROWS + 1]
        weighted = (x * spread[0:ROWS]).astype(BF16)
        state_ref[...] = dot(keyt[o // PER_GROUP], weighted).astype(BF16)
        decay_out[...] = spread[2 * ROWS - 1 : 2 * ROWS]

    def first_pass(k, c):
        o = lax.rem(me + k, ranks)
        local_state(o, local_send.at[o], decay_send.at[o])
        remote(local_send.at[o], local_recv.at[me], loc_sem.at[0], loc_sem.at[1], {"seq": o}).start()
        remote(decay_send.at[o], decay_recv.at[me], dec_sem.at[0], dec_sem.at[1], {"seq": o}).start()
        return c

    lax.fori_loop(1, ranks, first_pass, 0)
    local_state(me, local_recv.at[me], decay_recv.at[me])

    ones_row = lax.rem(lax.broadcasted_iota(jnp.int32, (2 * LANES, 2 * LANES), 0), HEADS)
    ones_half = lax.broadcasted_iota(jnp.int32, (2 * LANES, 2 * LANES), 1) // LANES

    def inside(o, c):
        pick = jnp.where(ones_row == ones_half + 2 * o, 1.0, 0.0).astype(BF16)
        spread = dot(cparts[...], pick)
        score = scores[o // PER_GROUP]
        x = xs[o]
        zero = jnp.zeros_like(x)
        total = vals[o]
        for half in range(2):
            spot = spread[:, half * LANES : (half + 1) * LANES] + logdt[pl.ds(2 * o + half, 1), :]
            weights = jnp.exp2(jnp.minimum(spot, 64.0)) * score
            mine = jnp.where(low_half if half == 0 else jnp.logical_not(low_half), x, zero)
            total = total + dot(weights.astype(BF16), mine)
        vals[o] = total
        return c

    lax.fori_loop(0, TILES, inside, 0)

    most = local_recv.at[pl.ds(0, ranks - 1)]
    pltpu.make_async_copy(most, most, loc_sem.at[1]).wait()
    most_decay = decay_recv.at[pl.ds(0, ranks - 1)]
    pltpu.make_async_copy(most_decay, most_decay, dec_sem.at[1]).wait()

    def carry(s, state):
        state_send[s] = state.astype(BF16)
        return state * decay_recv[s] + local_recv[s].astype(F32)

    lax.fori_loop(0, ranks, carry, jnp.zeros((LANES, LANES), F32))

    def send_state(k, c):
        s = lax.rem(me + k, ranks)
        remote(state_send.at[s], state_recv.at[me], st_send_sem, st_recv_sem.at[me], {"seq": s}).start()
        return c

    lax.fori_loop(1, ranks, send_state, 0)
    square[...] = jnp.zeros_like(square)

    def finish(o, state):
        g = o // PER_GROUP
        value = (vals[o] + dot(query[g], state) * expc[o]) * gates[o].astype(F32)
        vals[o] = value
        square[g] = square[g] + value * value

    finish(me, state_send[me])

    def arrive(k, c):
        o = lax.rem(me + ranks - k, ranks)
        slot = state_recv.at[o]
        pltpu.make_async_copy(slot, slot, st_recv_sem.at[o]).wait()
        finish(o, state_recv[o])
        return c

    lax.fori_loop(1, ranks, arrive, 0)

    writes = []
    for g in range(GROUPS):
        mean = jnp.sum(square[g], axis=1, keepdims=True) * (1.0 / (PER_GROUP * LANES))
        inverse = lax.rsqrt(mean + EPS)
        for j in range(PER_GROUP):
            o = g * PER_GROUP + j
            out_v[:, o * LANES : (o + 1) * LANES] = (
                vals[o] * inverse * gfull[:, o * LANES : (o + 1) * LANES]
            ).astype(BF16)
        part = slice(g * 1024, (g + 1) * 1024)
        write = pltpu.make_async_copy(out_v.at[:, part], out_hbm.at[0, :, part], out_sem.at[g])
        write.start()
        writes.append(write)

    pltpu.make_async_copy(several, several, par_sem.at[0]).wait()
    pltpu.make_async_copy(most, most, loc_sem.at[0]).wait()
    pltpu.make_async_copy(most_decay, most_decay, dec_sem.at[0]).wait()
    sent = state_send.at[pl.ds(0, ranks - 1)]
    pltpu.make_async_copy(sent, sent, st_send_sem).wait()
    for write in writes:
        write.wait()


def mixer(ranks, shards, *operands):
    tile = (TILES, ROWS, LANES)
    pair = (ranks, LANES, LANES)
    row = (ranks, 1, LANES)
    dma = pltpu.SemaphoreType.DMA
    whole = pl.BlockSpec(memory_space=pltpu.VMEM)
    scalars = pl.BlockSpec(memory_space=pltpu.SMEM)
    far = pl.BlockSpec(memory_space=pl.ANY)
    return pl.pallas_call(
        functools.partial(kernel, ranks, shards),
        out_shape=jax.ShapeDtypeStruct((1, ROWS, INNER), BF16),
        in_specs=[far, far, far, whole, whole, scalars, scalars, scalars, whole],
        out_specs=far,
        scratch_shapes=[
            pltpu.VMEM((ROWS, CONV_DIM), BF16),
            pltpu.VMEM((ROWS, INNER), BF16),
            pltpu.VMEM((HEADS, ROWS), BF16),
            pltpu.VMEM((16, CONV_DIM), BF16),
            pltpu.VMEM((16, 1024), F32),
            pltpu.VMEM((16, 1024), BF16),
            pltpu.VMEM((16, 1024), BF16),
            pltpu.VMEM((8, CONV_DIM), F32),
            pltpu.VMEM((8, 384), F32),
            pltpu.VMEM((shards, 8, 384), F32),
            pltpu.VMEM((8, CONV_DIM), F32),
            pltpu.VMEM((1, INNER), F32),
            pltpu.VMEM((2 * ROWS + 16, 2 * LANES), BF16),
            pltpu.VMEM((ROWS, 2 * LANES), BF16),
            pltpu.VMEM((LANES, ROWS), F32),
            pltpu.VMEM((GROUPS, LANES, ROWS), BF16),
            pltpu.VMEM((GROUPS, ROWS, LANES), BF16),
            pltpu.VMEM((GROUPS, ROWS, ROWS), F32),
            pltpu.VMEM(tile, BF16),
            pltpu.VMEM(tile, F32),
            pltpu.VMEM(tile, F32),
            pltpu.VMEM(tile, F32),
            pltpu.VMEM((GROUPS, ROWS, LANES), F32),
            pltpu.VMEM((ROWS, INNER), BF16),
            pltpu.VMEM(pair, BF16),
            pltpu.VMEM(pair, BF16),
            pltpu.VMEM(row, F32),
            pltpu.VMEM(row, F32),
            pltpu.VMEM(pair, BF16),
            pltpu.VMEM(pair, BF16),
            dma((4,)),
            dma((GROUPS,)),
            dma((2,)),
            dma((2,)),
            dma((2,)),
            dma((2,)),
            dma,
            dma((ranks,)),
        ],
        compiler_params=pltpu.CompilerParams(
            collective_id=0, has_side_effects=True, vmem_limit_bytes=40 * 1024 * 1024
        ),
        name="mixer",
    )(*operands)


def solution(mesh):
    ranks, shards = mesh.shape["seq"], mesh.shape["fsdp"]

    def body(conv_input, gate_input, step_input, conv_weight, conv_bias, decay_log, step_bias, skip_weight, norm_gain):
        return mixer(
            ranks, shards, conv_input, gate_input, jnp.swapaxes(step_input, 1, 2),
            conv_weight, conv_bias, decay_log, step_bias, skip_weight, norm_gain,
        )

    return jax.shard_map(
        body,
        mesh=mesh,
        in_specs=(
            P("fsdp", "seq", None),
            P("fsdp", "seq", None),
            P("fsdp", "seq", None),
            P(None, "fsdp"),
            P("fsdp"),
            P("fsdp"),
            P("fsdp"),
            P("fsdp"),
            P("fsdp"),
        ),
        out_specs=P("fsdp", "seq", None),
        check_vma=False,
    )
```

```python
import functools

import jax
import jax.numpy as jnp
from jax import lax
from jax.experimental import pallas as pl
from jax.experimental.pallas import tpu as pltpu
from jax.sharding import PartitionSpec as P

HEADS = 64
GROUPS = 4
KERNEL = 4
INNER = 4096
CONV_DIM = 5120
EPS = 1e-05
ROWS = 128
LANES = 128
TILES = INNER // LANES
PER_GROUP = TILES // GROUPS
LOG2E = 1.4426950408889634
SIDE = 4
CHUNKS = 4
OFFSETS = (
    ((1, 1), (7, 3), (1, 3), (7, 1)),
    ((2, 1), (6, 3), (2, 3), (6, 1)),
    ((3, 1), (5, 3), (3, 3), (5, 1)),
    ((1, 0), (7, 0), (0, 1), (0, 3)),
    ((2, 0), (6, 0), (0, 2), (4, 0)),
    ((3, 0), (5, 0), (4, 1), (4, 3)),
    ((2, 2), (6, 2), (3, 2), (5, 2)),
    ((1, 2), (7, 2), (4, 2), (0, 0)),
)
MESH = pl.DeviceIdType.MESH
F32 = jnp.float32
BF16 = jnp.bfloat16


def dot(a, b):
    return jnp.dot(a, b, preferred_element_type=F32)


def silu(v):
    half = 0.5 * v
    return half + half * jnp.tanh(half)


def three_parts(v):
    top = v.astype(BF16).astype(F32)
    rest = v - top
    middle = rest.astype(BF16).astype(F32)
    return top, middle, rest - middle


def remote(src, dst, send, recv, device):
    return pltpu.make_async_remote_copy(
        src_ref=src, dst_ref=dst, send_sem=send, recv_sem=recv,
        device_id=device, device_id_type=MESH,
    )


def packed(group):
    code = 0
    for along_z, along_y in reversed(group):
        code = code * 32 + along_z * SIDE + along_y
    return code


def for_groups(step):
    def one(_, codes):
        first = codes[0]
        step([lax.rem(lax.div(first, 32**i), 32) for i in range(4)])
        return codes[1:] + codes[:1]

    lax.fori_loop(0, len(OFFSETS), one, tuple(jnp.int32(packed(group)) for group in OFFSETS))


def shifted(rank, offset, ranks, sign=1):
    high = ranks // SIDE
    z = lax.rem(lax.div(rank, SIDE) + high + sign * lax.div(offset, SIDE), high)
    y = lax.rem(lax.rem(rank, SIDE) + SIDE + sign * lax.rem(offset, SIDE), SIDE)
    return z * SIDE + y


def kernel(
    ranks, shards,
    conv_hbm, gate_hbm, step_hbm, weight_hbm, bias_hbm, decay_hbm, step_bias_hbm, skip_hbm, gain_hbm,
    out_ref,
    weight_ref, bias_ref, decay_ref, step_bias_ref, skip_ref, gain_ref,
    conv_v, gate_v, step_v, tail_v, halo_pack, halo_send, halo_recv, halo,
    par_send, par, wfull, gfull,
    wide, cparts, logdt, keyt, query, scores,
    xs, vals, expc, gates, square,
    local_send, local_recv, decay_send, decay_recv, state_send, state_recv,
    load_sem, halo_sem, par_sem, loc_sem, dec_sem, st_send_sem, st_recv_sem,
):
    me = lax.axis_index("seq")
    shard = lax.axis_index("fsdp")

    def load(src, dst, slot):
        return pltpu.make_async_copy(src, dst, load_sem.at[slot])

    tail_load = load(conv_hbm.at[0, pl.ds(ROWS - 16, 16)], tail_v, 0)
    step_load = load(step_hbm.at[0], step_v, 1)
    conv_load = load(conv_hbm.at[0], conv_v, 2)
    gate_load = load(gate_hbm.at[0], gate_v, 3)
    small_loads = [
        load(src, dst, 4 + i)
        for i, (src, dst) in enumerate((
            (weight_hbm, weight_ref), (bias_hbm, bias_ref), (gain_hbm, gain_ref),
            (decay_hbm, decay_ref), (step_bias_hbm, step_bias_ref), (skip_hbm, skip_ref),
        ))
    ]
    for small_load in small_loads:
        small_load.start()
    tail_load.start()
    step_load.start()
    conv_load.start()
    gate_load.start()

    barrier = pltpu.get_barrier_semaphore()

    def greet_rank(k, c):
        pl.semaphore_signal(barrier, inc=1, device_id={"seq": lax.rem(me + k, ranks)}, device_id_type=MESH)
        return c

    def greet_shard(k, c):
        pl.semaphore_signal(barrier, inc=1, device_id={"fsdp": lax.rem(shard + k, shards)}, device_id_type=MESH)
        return c

    lax.fori_loop(1, shards, greet_shard, 0)
    lax.fori_loop(1, ranks, greet_rank, 0)

    width = CONV_DIM // shards
    heads = HEADS // shards
    par_send[...] = jnp.zeros_like(par_send)
    for small_load in small_loads:
        small_load.wait()
    odd = lax.rem(shard, 2)

    @pl.when(odd == 0)
    def _():
        par_send[0:4, 0:width] = weight_ref[...]
        par_send[4:5, 0:width] = bias_ref[...].reshape(1, width)

    @pl.when(odd == 1)
    def _():
        par_send[0:4, 64 : 64 + width] = weight_ref[...]
        par_send[4:5, 64 : 64 + width] = bias_ref[...].reshape(1, width)

    par_send[5:6, 0:256] = gain_ref[...].reshape(1, 256)
    lane = lax.broadcasted_iota(jnp.int32, (1, LANES), 1)
    for place, ref in enumerate((decay_ref, step_bias_ref, skip_ref)):
        row = jnp.zeros((1, LANES), F32)
        for h in range(heads):
            row = jnp.where(lane == shard * heads + h, ref[h], row)
            row = jnp.where(lane == HEADS + shard * heads + h, ref[h], row)
        par_send[6:7, place * LANES : (place + 1) * LANES] = row

    tail_load.wait()
    halo_pack[15:16, :] = jnp.zeros((1, 1024), F32)
    tail = tail_v[...].astype(F32)
    for r in range(KERNEL - 1):
        for c in range(CONV_DIM // 1024):
            halo_pack[r * 5 + c : r * 5 + c + 1, :] = tail[13 + r : 14 + r, c * 1024 : (c + 1) * 1024]
    halo_send[...] = halo_pack[...].astype(BF16)

    pl.semaphore_wait(barrier, ranks + shards - 2)

    halo_copy = remote(halo_send, halo_recv, halo_sem.at[0], halo_sem.at[1], {"seq": lax.rem(me + 1, ranks)})
    halo_copy.start()

    def send_par(k, c):
        remote(par_send, par.at[shard], par_sem.at[0], par_sem.at[1],
               {"fsdp": lax.rem(shard + k, shards)}).start()
        return c

    lax.fori_loop(1, shards, send_par, 0)
    par[shard] = par_send[...]

    gate_load.wait()

    def gate_tile(o, c):
        at = pl.ds(pl.multiple_of(o * LANES, LANES), LANES)
        gates[o] = silu(gate_v[:, at].astype(F32)).astype(gates.dtype)
        return c

    lax.fori_loop(0, TILES, gate_tile, 0)
    conv_load.wait()
    step_load.wait()

    several = par.at[pl.ds(0, shards - 1)]
    pltpu.make_async_copy(several, several, par_sem.at[1]).wait()
    for j in range(shards // 2):
        left, right = par[2 * j], par[2 * j + 1]
        at = 5 * j * LANES
        wfull[:, at : at + 256] = left[:, 0:256]
        wfull[:, at + 256 : at + 384] = left[:, 256:384] + right[:, 0:128]
        wfull[:, at + 384 : at + 640] = right[:, 128:384]
    small = jnp.zeros((1, 3 * LANES), F32)
    for i in range(shards):
        gfull[:, i * 256 : (i + 1) * 256] = par[i, 5:6, 0:256]
        small = small + par[i, 6:7, :]
    decay_row, bias_row, skip_row = (small[:, i * LANES : (i + 1) * LANES] for i in range(3))

    halo_copy.wait()
    before = jnp.where(me == 0, 0.0, halo_recv[...].astype(F32))
    for r in range(KERNEL - 1):
        for c in range(CONV_DIM // 1024):
            halo[5 + r : 6 + r, c * 1024 : (c + 1) * 1024] = before[r * 5 + c : r * 5 + c + 1, :]

    def convolved(at):
        rows = jnp.concatenate([halo[:, at], conv_v[:, at].astype(F32)], axis=0)
        taps = wfull[:, at]
        total = taps[4:5] + taps[3:4] * rows[8:]
        for back in range(1, KERNEL):
            total = total + taps[3 - back : 4 - back] * pltpu.roll(rows, back, 0)[8:]
        return silu(total)

    step = step_v[...].astype(F32)
    step = jnp.concatenate([step, step], axis=0).T
    dt = jax.nn.softplus(step + bias_row)
    after = lax.broadcasted_iota(jnp.int32, (ROWS, ROWS), 0)
    ahead = lax.broadcasted_iota(jnp.int32, (ROWS, ROWS), 1)
    causal = after >= ahead
    lower = jnp.where(causal, 1.0, 0.0)
    rate2 = -jnp.exp(decay_row) * LOG2E
    cumul = jnp.dot(lower, dt * rate2, precision=lax.Precision.HIGHEST, preferred_element_type=F32)
    low_half = lax.broadcasted_iota(jnp.int32, (ROWS, LANES), 1) < HEADS

    def spread_parts(v):
        top, middle, low = three_parts(v)
        first = jnp.where(low_half[: v.shape[0]], top, middle)
        return first.astype(BF16), jnp.where(low_half[: v.shape[0]], low, 0.0).astype(BF16)

    cparts[:, 0:LANES], cparts[:, LANES:] = spread_parts(cumul)
    logdt[...] = jnp.log2(dt).T - cumul.T
    wide[0:ROWS, 0:LANES], wide[0:ROWS, LANES:] = spread_parts(dt * jnp.exp2(cumul[ROWS - 1 : ROWS] - cumul))
    wide[ROWS : 2 * ROWS, 0:LANES], wide[ROWS : 2 * ROWS, LANES:] = spread_parts(jnp.exp2(cumul))
    skip16 = jnp.broadcast_to(skip_row, (16, LANES))
    wide[2 * ROWS :, 0:LANES], wide[2 * ROWS :, LANES:] = spread_parts(skip16)

    for g in range(GROUPS):
        keys = convolved(slice(INNER + g * LANES, INNER + (g + 1) * LANES))
        keyt[g] = keys.T.astype(BF16)
        asked = convolved(slice(INNER + (GROUPS + g) * LANES, INNER + (GROUPS + g + 1) * LANES))
        query[g] = asked.astype(BF16)
        scores[g] = jnp.where(causal, dot(query[g], keyt[g]), 0.0)

    pick_row = lax.rem(lax.broadcasted_iota(jnp.int32, (2 * LANES, LANES), 0), HEADS)
    pick_half = lax.broadcasted_iota(jnp.int32, (2 * LANES, LANES), 1) // HEADS

    def local_state(o, state_ref, decay_out):
        at = pl.ds(pl.multiple_of(o * LANES, LANES), LANES)
        x = convolved(at)
        pick = jnp.where(pick_row == pick_half + 2 * o, 1.0, 0.0).astype(BF16)
        spread = dot(wide[...], pick)
        expc[o] = spread[ROWS : 2 * ROWS]
        xs[o] = x.astype(BF16)
        vals[o] = x * spread[2 * ROWS : 2 * ROWS + 1]
        weighted = (x * spread[0:ROWS]).astype(BF16)
        state_ref[...] = dot(keyt[lax.div(o, PER_GROUP)], weighted).astype(BF16)
        decay_out[...] = spread[2 * ROWS - 1 : 2 * ROWS]

    tall = LANES // CHUNKS

    def send_tiles(targets, offsets, src, dst, send_sem, recv_sem):
        for c in range(CHUNKS):
            for target, offset in zip(targets, offsets):

                @pl.when(offset != 0)
                def _():
                    rows = pl.ds(c * tall, tall)
                    remote(src.at[target, rows], dst.at[me, rows], send_sem, recv_sem, {"seq": target}).start()

    def first_pass(offsets):
        targets = [shifted(me, offset, ranks) for offset in offsets]
        for target, offset in zip(targets, offsets):
            local_state(target, local_send.at[target], decay_send.at[target])

            @pl.when(offset != 0)
            def _():
                remote(decay_send.at[target], decay_recv.at[me], dec_sem.at[0], dec_sem.at[1], {"seq": target}).start()

        send_tiles(targets, offsets, local_send, local_recv, loc_sem.at[0], loc_sem.at[1])

    for_groups(first_pass)
    local_recv[me] = local_send[me]
    decay_recv[me] = decay_send[me]

    ones_row = lax.rem(lax.broadcasted_iota(jnp.int32, (2 * LANES, 2 * LANES), 0), HEADS)
    ones_half = lax.broadcasted_iota(jnp.int32, (2 * LANES, 2 * LANES), 1) // LANES

    def inside(o, c):
        pick = jnp.where(ones_row == ones_half + 2 * o, 1.0, 0.0).astype(BF16)
        spread = dot(cparts[...], pick)
        score = scores[lax.div(o, PER_GROUP)]
        x = xs[o]
        zero = jnp.zeros_like(x)
        total = vals[o]
        for half in range(2):
            spot = spread[:, half * LANES : (half + 1) * LANES] + logdt[pl.ds(2 * o + half, 1), :]
            weights = jnp.exp2(jnp.minimum(spot, 64.0)) * score
            mine = jnp.where(low_half if half == 0 else jnp.logical_not(low_half), x, zero)
            total = total + dot(weights.astype(BF16), mine)
        vals[o] = total
        return c

    lax.fori_loop(0, TILES, inside, 0)

    most = local_recv.at[pl.ds(0, ranks - 1)]
    pltpu.make_async_copy(most, most, loc_sem.at[1]).wait()
    most_decay = decay_recv.at[pl.ds(0, ranks - 1)]
    pltpu.make_async_copy(most_decay, most_decay, dec_sem.at[1]).wait()

    def carry(s, state):
        state_send[s] = state.astype(BF16)
        return state * decay_recv[s] + local_recv[s].astype(F32)

    lax.fori_loop(0, ranks, carry, jnp.zeros((LANES, LANES), F32))

    def second_pass(offsets):
        targets = [shifted(me, offset, ranks) for offset in offsets]
        send_tiles(targets, offsets, state_send, state_recv, st_send_sem, st_recv_sem.at[me])

    for_groups(second_pass)
    state_recv[me] = state_send[me]
    square[...] = jnp.zeros_like(square)

    def arrive(offsets):
        for offset in offsets:
            o = shifted(me, offset, ranks, -1)

            @pl.when(offset != 0)
            def _():
                slot = state_recv.at[o]
                pltpu.make_async_copy(slot, slot, st_recv_sem.at[o]).wait()

            g = lax.div(o, PER_GROUP)
            value = (vals[o] + dot(query[g], state_recv[o]) * expc[o]) * gates[o].astype(F32)
            vals[o] = value
            square[g] = square[g] + value * value

    for_groups(arrive)

    for g in range(GROUPS):
        mean = jnp.sum(square[g], axis=1, keepdims=True) * (1.0 / (PER_GROUP * LANES))
        inverse = lax.rsqrt(mean + EPS)
        for j in range(PER_GROUP):
            o = g * PER_GROUP + j
            out_ref[0, :, o * LANES : (o + 1) * LANES] = (
                vals[o] * inverse * gfull[:, o * LANES : (o + 1) * LANES]
            ).astype(BF16)

    pltpu.make_async_copy(several, several, par_sem.at[0]).wait()
    pltpu.make_async_copy(most, most, loc_sem.at[0]).wait()
    pltpu.make_async_copy(most_decay, most_decay, dec_sem.at[0]).wait()
    sent = state_send.at[pl.ds(0, ranks - 1)]
    pltpu.make_async_copy(sent, sent, st_send_sem).wait()


def mixer(ranks, shards, *operands):
    tile = (TILES, ROWS, LANES)
    pair = (ranks, LANES, LANES)
    row = (ranks, 1, LANES)
    dma = pltpu.SemaphoreType.DMA
    far = pl.BlockSpec(memory_space=pl.ANY)
    return pl.pallas_call(
        functools.partial(kernel, ranks, shards),
        out_shape=pltpu.VMEM((1, ROWS, INNER), BF16),
        in_specs=[far] * 9,
        out_specs=pl.BlockSpec(memory_space=pltpu.VMEM),
        scratch_shapes=[
            pltpu.VMEM((KERNEL, CONV_DIM // shards), F32),
            pltpu.VMEM((CONV_DIM // shards,), F32),
            pltpu.SMEM((HEADS // shards,), F32),
            pltpu.SMEM((HEADS // shards,), F32),
            pltpu.SMEM((HEADS // shards,), F32),
            pltpu.VMEM((INNER // shards,), F32),
            pltpu.VMEM((ROWS, CONV_DIM), BF16),
            pltpu.VMEM((ROWS, INNER), BF16),
            pltpu.VMEM((HEADS, ROWS), BF16),
            pltpu.VMEM((16, CONV_DIM), BF16),
            pltpu.VMEM((16, 1024), F32),
            pltpu.VMEM((16, 1024), BF16),
            pltpu.VMEM((16, 1024), BF16),
            pltpu.VMEM((8, CONV_DIM), F32),
            pltpu.VMEM((8, 384), F32),
            pltpu.VMEM((shards, 8, 384), F32),
            pltpu.VMEM((8, CONV_DIM), F32),
            pltpu.VMEM((1, INNER), F32),
            pltpu.VMEM((2 * ROWS + 16, 2 * LANES), BF16),
            pltpu.VMEM((ROWS, 2 * LANES), BF16),
            pltpu.VMEM((LANES, ROWS), F32),
            pltpu.VMEM((GROUPS, LANES, ROWS), BF16),
            pltpu.VMEM((GROUPS, ROWS, LANES), BF16),
            pltpu.VMEM((GROUPS, ROWS, ROWS), F32),
            pltpu.VMEM(tile, BF16),
            pltpu.VMEM(tile, F32),
            pltpu.VMEM(tile, F32),
            pltpu.VMEM(tile, F32),
            pltpu.VMEM((GROUPS, ROWS, LANES), F32),
            pltpu.VMEM(pair, BF16),
            pltpu.VMEM(pair, BF16),
            pltpu.VMEM(row, F32),
            pltpu.VMEM(row, F32),
            pltpu.VMEM(pair, BF16),
            pltpu.VMEM(pair, BF16),
            dma((10,)),
            dma((2,)),
            dma((2,)),
            dma((2,)),
            dma((2,)),
            dma,
            dma((ranks,)),
        ],
        compiler_params=pltpu.CompilerParams(
            collective_id=0, has_side_effects=True, vmem_limit_bytes=60 * 1024 * 1024
        ),
        name="mixer",
    )(*operands)


def solution(mesh):
    ranks, shards = mesh.shape["seq"], mesh.shape["fsdp"]

    def body(conv_input, gate_input, step_input, conv_weight, conv_bias, decay_log, step_bias, skip_weight, norm_gain):
        return mixer(
            ranks, shards, conv_input, gate_input, jnp.swapaxes(step_input, 1, 2),
            conv_weight, conv_bias, decay_log, step_bias, skip_weight, norm_gain,
        )

    return jax.shard_map(
        body,
        mesh=mesh,
        in_specs=(
            P("fsdp", "seq", None),
            P("fsdp", "seq", None),
            P("fsdp", "seq", None),
            P(None, "fsdp"),
            P("fsdp"),
            P("fsdp"),
            P("fsdp"),
            P("fsdp"),
            P("fsdp"),
        ),
        out_specs=P("fsdp", "seq", None),
        check_vma=False,
    )
```

```python
import functools

import jax
import jax.numpy as jnp
from jax import lax
from jax.experimental import pallas as pl
from jax.experimental.pallas import tpu as pltpu
from jax.sharding import PartitionSpec as P

HEADS = 64
GROUPS = 4
KERNEL = 4
INNER = 4096
CONV_DIM = 5120
EPS = 1e-05
ROWS = 128
LANES = 128
TILES = INNER // LANES
PER_GROUP = TILES // GROUPS
LOG2E = 1.4426950408889634
INSIDE_FIRST = 12
SIDE = 4
PIECES = 2
CHUNKS = 4
OFFSETS = (
    ((3, 0), (5, 0), (1, 2), (7, 2)),
    ((2, 1), (6, 3), (2, 3), (6, 1)),
    ((2, 0), (6, 0), (2, 2), (6, 2)),
    ((1, 1), (7, 3), (3, 3), (5, 1)),
    ((1, 0), (7, 0), (3, 2), (5, 2)),
    ((1, 3), (7, 1), (3, 1), (5, 3)),
    ((0, 1), (0, 3), (4, 0), (4, 2)),
    ((4, 1), (4, 3), (0, 2), (0, 0)),
)
MESH = pl.DeviceIdType.MESH
F32 = jnp.float32
BF16 = jnp.bfloat16


def dot(a, b):
    return jnp.dot(a, b, preferred_element_type=F32)


def silu(v):
    half = 0.5 * v
    return half + half * jnp.tanh(half)


def three_parts(v):
    top = v.astype(BF16).astype(F32)
    rest = v - top
    middle = rest.astype(BF16).astype(F32)
    return top, middle, rest - middle


def remote(src, dst, send, recv, device):
    return pltpu.make_async_remote_copy(
        src_ref=src, dst_ref=dst, send_sem=send, recv_sem=recv,
        device_id=device, device_id_type=MESH,
    )


def packed(group):
    code = 0
    for along_z, along_y in reversed(group):
        code = code * 32 + along_z * SIDE + along_y
    return code


def for_groups(step):
    def one(_, codes):
        first = codes[0]
        step([lax.rem(lax.div(first, 32**i), 32) for i in range(4)])
        return codes[1:] + codes[:1]

    lax.fori_loop(0, len(OFFSETS), one, tuple(jnp.int32(packed(group)) for group in OFFSETS))


def shifted(rank, offset, ranks, sign=1):
    high = ranks // SIDE
    z = lax.rem(lax.div(rank, SIDE) + high + sign * lax.div(offset, SIDE), high)
    y = lax.rem(lax.rem(rank, SIDE) + SIDE + sign * lax.rem(offset, SIDE), SIDE)
    return z * SIDE + y


def kernel(
    ranks, shards,
    conv_hbm, gate_hbm, step_hbm, weight_hbm, bias_hbm, decay_hbm, step_bias_hbm, skip_hbm, gain_hbm,
    out_ref,
    weight_ref, bias_ref, decay_ref, step_bias_ref, skip_ref, gain_ref,
    conv_v, gate_v, step_v, tail_v, halo_pack, halo_send, halo_recv, halo,
    par_send, par, wfull, gfull,
    wide, cparts, logdt, keyt, query, scores,
    xs, vals, expc, gates, square,
    local_send, local_recv, decay_send, decay_recv, state_send, state_recv,
    load_sem, ready, halo_sem, par_sem, loc_sem, dec_sem, st_send_sem, st_recv_sem,
):
    me = lax.axis_index("seq")
    shard = lax.axis_index("fsdp")

    def load(src, dst, slot):
        return pltpu.make_async_copy(src, dst, load_sem.at[slot])

    tail_load = load(conv_hbm.at[0, pl.ds(ROWS - 16, 16)], tail_v, 0)
    step_load = load(step_hbm.at[0], step_v, 1)
    conv_load = load(conv_hbm.at[0], conv_v, 2)
    gate_load = load(gate_hbm.at[0], gate_v, 3)
    small_loads = [
        load(src, dst, 4 + i)
        for i, (src, dst) in enumerate((
            (weight_hbm, weight_ref), (bias_hbm, bias_ref), (gain_hbm, gain_ref),
            (decay_hbm, decay_ref), (step_bias_hbm, step_bias_ref), (skip_hbm, skip_ref),
        ))
    ]
    for small_load in small_loads:
        small_load.start()
    tail_load.start()
    step_load.start()
    conv_load.start()
    gate_load.start()

    barrier = pltpu.get_barrier_semaphore()

    def greet_shard(k, c):
        pl.semaphore_signal(barrier, inc=1, device_id={"fsdp": lax.rem(shard + k, shards)}, device_id_type=MESH)
        return c

    def greet_rank(offset, c):
        pl.semaphore_signal(barrier, inc=1, device_id={"seq": shifted(me, offset, ranks)}, device_id_type=MESH)
        return c

    high = ranks // SIDE
    lax.fori_loop(1, shards, greet_shard, 0)
    lax.fori_loop(1, SIDE, greet_rank, 0)
    lax.fori_loop(1, high, lambda k, c: greet_rank(k * SIDE, c), 0)

    width = CONV_DIM // shards
    heads = HEADS // shards
    par_send[...] = jnp.zeros_like(par_send)
    for small_load in small_loads:
        small_load.wait()
    odd = lax.rem(shard, 2)

    @pl.when(odd == 0)
    def _():
        par_send[0:4, 0:width] = weight_ref[...]
        par_send[4:5, 0:width] = bias_ref[...].reshape(1, width)

    @pl.when(odd == 1)
    def _():
        par_send[0:4, 64 : 64 + width] = weight_ref[...]
        par_send[4:5, 64 : 64 + width] = bias_ref[...].reshape(1, width)

    par_send[5:6, 0:256] = gain_ref[...].reshape(1, 256)
    lane = lax.broadcasted_iota(jnp.int32, (1, LANES), 1)
    for place, ref in enumerate((decay_ref, step_bias_ref, skip_ref)):
        row = jnp.zeros((1, LANES), F32)
        for h in range(heads):
            row = jnp.where(lane == shard * heads + h, ref[h], row)
            row = jnp.where(lane == HEADS + shard * heads + h, ref[h], row)
        par_send[6:7, place * LANES : (place + 1) * LANES] = row

    tail_load.wait()
    halo_pack[15:16, :] = jnp.zeros((1, 1024), F32)
    tail = tail_v[...].astype(F32)
    for r in range(KERNEL - 1):
        for c in range(CONV_DIM // 1024):
            halo_pack[r * 5 + c : r * 5 + c + 1, :] = tail[13 + r : 14 + r, c * 1024 : (c + 1) * 1024]
    halo_send[...] = halo_pack[...].astype(BF16)

    pl.semaphore_wait(barrier, shards - 1 + SIDE - 1 + high - 1)

    def send_par(k, c):
        remote(par_send, par.at[shard], par_sem.at[0], par_sem.at[1],
               {"fsdp": lax.rem(shard + k, shards)}).start()
        return c

    def tell(offset, c):
        pl.semaphore_signal(ready, inc=1, device_id={"seq": shifted(me, offset, ranks)}, device_id_type=MESH)
        return c

    lax.fori_loop(1, SIDE, tell, 0)
    lax.fori_loop(1, shards, send_par, 0)
    pl.semaphore_wait(ready, SIDE - 1)
    halo_copy = remote(halo_send, halo_recv, halo_sem.at[0], halo_sem.at[1], {"seq": lax.rem(me + 1, ranks)})
    halo_copy.start()

    par[shard] = par_send[...]

    gate_load.wait()

    def gate_tile(o, c):
        at = pl.ds(pl.multiple_of(o * LANES, LANES), LANES)
        gates[o] = silu(gate_v[:, at].astype(F32)).astype(gates.dtype)
        return c

    lax.fori_loop(0, TILES, gate_tile, 0)
    conv_load.wait()
    step_load.wait()

    several = par.at[pl.ds(0, shards - 1)]
    pltpu.make_async_copy(several, several, par_sem.at[1]).wait()
    for j in range(shards // 2):
        left, right = par[2 * j], par[2 * j + 1]
        at = 5 * j * LANES
        wfull[:, at : at + 256] = left[:, 0:256]
        wfull[:, at + 256 : at + 384] = left[:, 256:384] + right[:, 0:128]
        wfull[:, at + 384 : at + 640] = right[:, 128:384]
    small = jnp.zeros((1, 3 * LANES), F32)
    for i in range(shards):
        gfull[:, i * 256 : (i + 1) * 256] = par[i, 5:6, 0:256]
        small = small + par[i, 6:7, :]
    decay_row, bias_row, skip_row = (small[:, i * LANES : (i + 1) * LANES] for i in range(3))

    halo_copy.wait()
    before = jnp.where(me == 0, 0.0, halo_recv[...].astype(F32))
    for r in range(KERNEL - 1):
        for c in range(CONV_DIM // 1024):
            halo[5 + r : 6 + r, c * 1024 : (c + 1) * 1024] = before[r * 5 + c : r * 5 + c + 1, :]

    def convolved(at):
        rows = jnp.concatenate([halo[:, at], conv_v[:, at].astype(F32)], axis=0)
        taps = wfull[:, at]
        total = taps[4:5] + taps[3:4] * rows[8:]
        for back in range(1, KERNEL):
            total = total + taps[3 - back : 4 - back] * pltpu.roll(rows, back, 0)[8:]
        return silu(total)

    step = step_v[...].astype(F32)
    step = jnp.concatenate([step, step], axis=0).T
    dt = jax.nn.softplus(step + bias_row)
    after = lax.broadcasted_iota(jnp.int32, (ROWS, ROWS), 0)
    ahead = lax.broadcasted_iota(jnp.int32, (ROWS, ROWS), 1)
    causal = after >= ahead
    lower = jnp.where(causal, 1.0, 0.0)
    rate2 = -jnp.exp(decay_row) * LOG2E
    cumul = jnp.dot(lower, dt * rate2, precision=lax.Precision.HIGHEST, preferred_element_type=F32)
    low_half = lax.broadcasted_iota(jnp.int32, (ROWS, LANES), 1) < HEADS

    def spread_parts(v):
        top, middle, low = three_parts(v)
        first = jnp.where(low_half[: v.shape[0]], top, middle)
        return first.astype(BF16), jnp.where(low_half[: v.shape[0]], low, 0.0).astype(BF16)

    cparts[:, 0:LANES], cparts[:, LANES:] = spread_parts(cumul)
    logdt[...] = jnp.log2(dt).T - cumul.T
    wide[0:ROWS, 0:LANES], wide[0:ROWS, LANES:] = spread_parts(dt * jnp.exp2(cumul[ROWS - 1 : ROWS] - cumul))
    wide[ROWS : 2 * ROWS, 0:LANES], wide[ROWS : 2 * ROWS, LANES:] = spread_parts(jnp.exp2(cumul))
    skip16 = jnp.broadcast_to(skip_row, (16, LANES))
    wide[2 * ROWS :, 0:LANES], wide[2 * ROWS :, LANES:] = spread_parts(skip16)

    for g in range(GROUPS):
        keys = convolved(slice(INNER + g * LANES, INNER + (g + 1) * LANES))
        keyt[g] = keys.T.astype(BF16)
        asked = convolved(slice(INNER + (GROUPS + g) * LANES, INNER + (GROUPS + g + 1) * LANES))
        query[g] = asked.astype(BF16)
        scores[g] = jnp.where(causal, dot(query[g], keyt[g]), 0.0)

    pick_row = lax.rem(lax.broadcasted_iota(jnp.int32, (2 * LANES, LANES), 0), HEADS)
    pick_half = lax.broadcasted_iota(jnp.int32, (2 * LANES, LANES), 1) // HEADS

    def local_state(o, state_ref, decay_out):
        at = pl.ds(pl.multiple_of(o * LANES, LANES), LANES)
        x = convolved(at)
        pick = jnp.where(pick_row == pick_half + 2 * o, 1.0, 0.0).astype(BF16)
        spread = dot(wide[...], pick)
        expc[o] = spread[ROWS : 2 * ROWS]
        xs[o] = x.astype(BF16)
        vals[o] = x * spread[2 * ROWS : 2 * ROWS + 1]
        weighted = (x * spread[0:ROWS]).astype(BF16)
        state_ref[...] = dot(keyt[lax.div(o, PER_GROUP)], weighted).astype(BF16)
        decay_out[...] = spread[2 * ROWS - 1 : 2 * ROWS]

    part = LANES // PIECES
    tall = part // CHUNKS

    def send_tiles(piece, targets, offsets, src, dst, send_sem, recv_sem):
        for c in range(CHUNKS):
            for target, offset in zip(targets, offsets):

                @pl.when(offset != 0)
                def _():
                    rows = pl.ds(piece * part + c * tall, tall)
                    remote(src.at[target, rows], dst.at[me, rows], send_sem, recv_sem, {"seq": target}).start()

    def first_pass(offsets):
        targets = [shifted(me, offset, ranks) for offset in offsets]
        for target, offset in zip(targets, offsets):
            local_state(target, local_send.at[target], decay_send.at[target])

            @pl.when(offset != 0)
            def _():
                remote(decay_send.at[target], decay_recv.at[me], dec_sem.at[0], dec_sem.at[1], {"seq": target}).start()

        send_local(0, targets, offsets)

    def send_local(piece, targets, offsets):
        send_tiles(piece, targets, offsets, local_send, local_recv, loc_sem.at[PIECES], loc_sem.at[piece])

    for_groups(first_pass)
    for piece in range(1, PIECES):
        for_groups(lambda offsets: send_local(piece, [shifted(me, offset, ranks) for offset in offsets], offsets))
    local_recv[me] = local_send[me]
    decay_recv[me] = decay_send[me]

    ones_row = lax.rem(lax.broadcasted_iota(jnp.int32, (2 * LANES, 2 * LANES), 0), HEADS)
    ones_half = lax.broadcasted_iota(jnp.int32, (2 * LANES, 2 * LANES), 1) // LANES

    def inside(o, c):
        pick = jnp.where(ones_row == ones_half + 2 * o, 1.0, 0.0).astype(BF16)
        spread = dot(cparts[...], pick)
        score = scores[lax.div(o, PER_GROUP)]
        x = xs[o]
        zero = jnp.zeros_like(x)
        total = vals[o]
        for half in range(2):
            spot = spread[:, half * LANES : (half + 1) * LANES] + logdt[pl.ds(2 * o + half, 1), :]
            weights = jnp.exp2(jnp.minimum(spot, 64.0)) * score
            mine = jnp.where(low_half if half == 0 else jnp.logical_not(low_half), x, zero)
            total = total + dot(weights.astype(BF16), mine)
        vals[o] = total
        return c

    def send_states(piece):
        here = slice(piece * part, (piece + 1) * part)
        landed = local_recv.at[pl.ds(0, ranks - 1), here]
        pltpu.make_async_copy(landed, landed, loc_sem.at[piece]).wait()

        def carry(s, state):
            state_send[s, here] = state.astype(BF16)
            return state * decay_recv[s] + local_recv[s, here].astype(F32)

        lax.fori_loop(0, ranks, carry, jnp.zeros((part, LANES), F32), unroll=4)

        def second_pass(offsets):
            targets = [shifted(me, offset, ranks) for offset in offsets]
            send_tiles(piece, targets, offsets, state_send, state_recv, st_send_sem, st_recv_sem.at[me])

        for_groups(second_pass)

    most = local_recv.at[pl.ds(0, ranks - 1)]
    most_decay = decay_recv.at[pl.ds(0, ranks - 1)]
    lax.fori_loop(0, INSIDE_FIRST, inside, 0)
    pltpu.make_async_copy(most_decay, most_decay, dec_sem.at[1]).wait()
    send_states(0)
    lax.fori_loop(INSIDE_FIRST, TILES, inside, 0)
    for piece in range(1, PIECES):
        send_states(piece)
    state_recv[me] = state_send[me]
    square[...] = jnp.zeros_like(square)

    def arrive(offsets):
        for offset in offsets:
            o = shifted(me, offset, ranks, -1)

            @pl.when(offset != 0)
            def _():
                slot = state_recv.at[o]
                pltpu.make_async_copy(slot, slot, st_recv_sem.at[o]).wait()

            g = lax.div(o, PER_GROUP)
            value = (vals[o] + dot(query[g], state_recv[o]) * expc[o]) * gates[o].astype(F32)
            vals[o] = value
            square[g] = square[g] + value * value

    for_groups(arrive)

    for g in range(GROUPS):
        mean = jnp.sum(square[g], axis=1, keepdims=True) * (1.0 / (PER_GROUP * LANES))
        inverse = lax.rsqrt(mean + EPS)
        for j in range(PER_GROUP):
            o = g * PER_GROUP + j
            out_ref[0, :, o * LANES : (o + 1) * LANES] = (
                vals[o] * inverse * gfull[:, o * LANES : (o + 1) * LANES]
            ).astype(BF16)

    pltpu.make_async_copy(several, several, par_sem.at[0]).wait()
    pltpu.make_async_copy(most, most, loc_sem.at[PIECES]).wait()
    pltpu.make_async_copy(most_decay, most_decay, dec_sem.at[0]).wait()
    sent = state_send.at[pl.ds(0, ranks - 1)]
    pltpu.make_async_copy(sent, sent, st_send_sem).wait()


def mixer(ranks, shards, *operands):
    tile = (TILES, ROWS, LANES)
    pair = (ranks, LANES, LANES)
    row = (ranks, 1, LANES)
    dma = pltpu.SemaphoreType.DMA
    far = pl.BlockSpec(memory_space=pl.ANY)
    return pl.pallas_call(
        functools.partial(kernel, ranks, shards),
        out_shape=pltpu.VMEM((1, ROWS, INNER), BF16),
        in_specs=[far] * 9,
        out_specs=pl.BlockSpec(memory_space=pltpu.VMEM),
        scratch_shapes=[
            pltpu.VMEM((KERNEL, CONV_DIM // shards), F32),
            pltpu.VMEM((CONV_DIM // shards,), F32),
            pltpu.SMEM((HEADS // shards,), F32),
            pltpu.SMEM((HEADS // shards,), F32),
            pltpu.SMEM((HEADS // shards,), F32),
            pltpu.VMEM((INNER // shards,), F32),
            pltpu.VMEM((ROWS, CONV_DIM), BF16),
            pltpu.VMEM((ROWS, INNER), BF16),
            pltpu.VMEM((HEADS, ROWS), BF16),
            pltpu.VMEM((16, CONV_DIM), BF16),
            pltpu.VMEM((16, 1024), F32),
            pltpu.VMEM((16, 1024), BF16),
            pltpu.VMEM((16, 1024), BF16),
            pltpu.VMEM((8, CONV_DIM), F32),
            pltpu.VMEM((8, 384), F32),
            pltpu.VMEM((shards, 8, 384), F32),
            pltpu.VMEM((8, CONV_DIM), F32),
            pltpu.VMEM((1, INNER), F32),
            pltpu.VMEM((2 * ROWS + 16, 2 * LANES), BF16),
            pltpu.VMEM((ROWS, 2 * LANES), BF16),
            pltpu.VMEM((LANES, ROWS), F32),
            pltpu.VMEM((GROUPS, LANES, ROWS), BF16),
            pltpu.VMEM((GROUPS, ROWS, LANES), BF16),
            pltpu.VMEM((GROUPS, ROWS, ROWS), F32),
            pltpu.VMEM(tile, BF16),
            pltpu.VMEM(tile, F32),
            pltpu.VMEM(tile, F32),
            pltpu.VMEM(tile, F32),
            pltpu.VMEM((GROUPS, ROWS, LANES), F32),
            pltpu.VMEM(pair, BF16),
            pltpu.VMEM(pair, BF16),
            pltpu.VMEM(row, F32),
            pltpu.VMEM(row, F32),
            pltpu.VMEM(pair, BF16),
            pltpu.VMEM(pair, BF16),
            dma((10,)),
            pltpu.SemaphoreType.REGULAR,
            dma((2,)),
            dma((2,)),
            dma((PIECES + 1,)),
            dma((2,)),
            dma,
            dma((ranks,)),
        ],
        compiler_params=pltpu.CompilerParams(
            collective_id=0, has_side_effects=True, vmem_limit_bytes=60 * 1024 * 1024
        ),
        name="mixer",
    )(*operands)


def solution(mesh):
    ranks, shards = mesh.shape["seq"], mesh.shape["fsdp"]

    def body(conv_input, gate_input, step_input, conv_weight, conv_bias, decay_log, step_bias, skip_weight, norm_gain):
        return mixer(
            ranks, shards, conv_input, gate_input, jnp.swapaxes(step_input, 1, 2),
            conv_weight, conv_bias, decay_log, step_bias, skip_weight, norm_gain,
        )

    return jax.shard_map(
        body,
        mesh=mesh,
        in_specs=(
            P("fsdp", "seq", None),
            P("fsdp", "seq", None),
            P("fsdp", "seq", None),
            P(None, "fsdp"),
            P("fsdp"),
            P("fsdp"),
            P("fsdp"),
            P("fsdp"),
            P("fsdp"),
        ),
        out_specs=P("fsdp", "seq", None),
        check_vma=False,
    )
```

```python
import functools

import jax
import jax.numpy as jnp
from jax import lax
from jax.experimental import pallas as pl
from jax.experimental.pallas import tpu as pltpu
from jax.sharding import PartitionSpec as P

HEADS = 64
GROUPS = 4
KERNEL = 4
INNER = 4096
CONV_DIM = 5120
EPS = 1e-05
ROWS = 128
LANES = 128
TILES = INNER // LANES
PER_GROUP = TILES // GROUPS
LOG2E = 1.4426950408889634
INSIDE_FIRST = 12
SIDE = 4
PIECES = 2
CHUNKS = 4
OFFSETS = (
    ((3, 0), (5, 0), (1, 2), (7, 2)),
    ((2, 1), (6, 3), (2, 3), (6, 1)),
    ((2, 0), (6, 0), (2, 2), (6, 2)),
    ((1, 1), (7, 3), (3, 3), (5, 1)),
    ((1, 0), (7, 0), (3, 2), (5, 2)),
    ((1, 3), (7, 1), (3, 1), (5, 3)),
    ((0, 1), (0, 3), (4, 0), (4, 2)),
    ((4, 1), (4, 3), (0, 2), (0, 0)),
)
MESH = pl.DeviceIdType.MESH
F32 = jnp.float32
BF16 = jnp.bfloat16


def dot(a, b):
    return jnp.dot(a, b, preferred_element_type=F32)


def silu(v):
    half = 0.5 * v
    return half + half * jnp.tanh(half)


def three_parts(v):
    top = v.astype(BF16).astype(F32)
    rest = v - top
    middle = rest.astype(BF16).astype(F32)
    return top, middle, rest - middle


def remote(src, dst, send, recv, device):
    return pltpu.make_async_remote_copy(
        src_ref=src, dst_ref=dst, send_sem=send, recv_sem=recv,
        device_id=device, device_id_type=MESH,
    )


def packed(group):
    code = 0
    for along_z, along_y in reversed(group):
        code = code * 32 + along_z * SIDE + along_y
    return code


def for_groups(step):
    def one(_, codes):
        first = codes[0]
        step([lax.rem(lax.div(first, 32**i), 32) for i in range(4)])
        return codes[1:] + codes[:1]

    lax.fori_loop(0, len(OFFSETS), one, tuple(jnp.int32(packed(group)) for group in OFFSETS))


def shifted(rank, offset, ranks, sign=1):
    high = ranks // SIDE
    z = lax.rem(lax.div(rank, SIDE) + high + sign * lax.div(offset, SIDE), high)
    y = lax.rem(lax.rem(rank, SIDE) + SIDE + sign * lax.rem(offset, SIDE), SIDE)
    return z * SIDE + y


def kernel(
    ranks, shards,
    conv_hbm, gate_hbm, step_hbm, weight_hbm, bias_hbm, decay_hbm, step_bias_hbm, skip_hbm, gain_hbm,
    out_ref,
    weight_ref, bias_ref, decay_ref, step_bias_ref, skip_ref, gain_ref,
    conv_v, gate_v, step_v, tail_v, halo_pack, halo_send, halo_recv, halo,
    par_send, par, wfull, gfull,
    wide, cparts, logdt, keyt, query, scores,
    xs, vals, expc, gates, square,
    local_send, local_recv, decay_send, decay_recv, state_send, state_recv,
    load_sem, ready, halo_sem, par_sem, loc_sem, dec_sem, st_send_sem, st_recv_sem,
):
    me = lax.axis_index("seq")
    shard = lax.axis_index("fsdp")

    def load(src, dst, slot):
        return pltpu.make_async_copy(src, dst, load_sem.at[slot])

    tail_load = load(conv_hbm.at[0, pl.ds(ROWS - 16, 16)], tail_v, 0)
    step_load = load(step_hbm.at[0], step_v, 1)
    conv_load = load(conv_hbm.at[0], conv_v, 2)
    gate_load = load(gate_hbm.at[0], gate_v, 3)
    small_loads = [
        load(src, dst, 4 + i)
        for i, (src, dst) in enumerate((
            (weight_hbm, weight_ref), (bias_hbm, bias_ref), (gain_hbm, gain_ref),
            (decay_hbm, decay_ref), (step_bias_hbm, step_bias_ref), (skip_hbm, skip_ref),
        ))
    ]
    for small_load in small_loads:
        small_load.start()
    tail_load.start()
    step_load.start()
    conv_load.start()
    gate_load.start()

    barrier = pltpu.get_barrier_semaphore()

    beside = shifted(me, 1, ranks, 1)
    behind = shifted(me, 1, ranks, -1)
    own_low = lax.rem(lax.div(shard, 2), 2)

    def peer(k):
        other = lax.rem(shard + k, shards)
        return other, lax.rem(lax.div(other, 2), 2) - own_low

    def greet_shard(k, c):
        other, rise = peer(k)
        source = jnp.where(rise == -1, beside, me)
        pl.semaphore_signal(barrier, inc=1, device_id={"fsdp": other, "seq": source}, device_id_type=MESH)
        return c

    def greet_rank(offset, c):
        pl.semaphore_signal(barrier, inc=1, device_id={"seq": shifted(me, offset, ranks)}, device_id_type=MESH)
        return c

    high = ranks // SIDE
    lax.fori_loop(1, shards, greet_shard, 0)
    lax.fori_loop(1, SIDE, greet_rank, 0)
    lax.fori_loop(1, high, lambda k, c: greet_rank(k * SIDE, c), 0)

    along_y = lax.rem(me, SIDE)

    @pl.when(along_y == SIDE - 1)
    def _():
        greet_rank(SIDE + 1, 0)

    @pl.when(along_y == 0)
    def _():
        greet_rank((high - 1) * SIDE + SIDE - 1, 0)


    width = CONV_DIM // shards
    heads = HEADS // shards
    par_send[...] = jnp.zeros_like(par_send)
    for small_load in small_loads:
        small_load.wait()
    odd = lax.rem(shard, 2)

    @pl.when(odd == 0)
    def _():
        par_send[0:4, 0:width] = weight_ref[...]
        par_send[4:5, 0:width] = bias_ref[...].reshape(1, width)

    @pl.when(odd == 1)
    def _():
        par_send[0:4, 64 : 64 + width] = weight_ref[...]
        par_send[4:5, 64 : 64 + width] = bias_ref[...].reshape(1, width)

    par_send[5:6, 0:256] = gain_ref[...].reshape(1, 256)
    lane = lax.broadcasted_iota(jnp.int32, (1, LANES), 1)
    for place, ref in enumerate((decay_ref, step_bias_ref, skip_ref)):
        row = jnp.zeros((1, LANES), F32)
        for h in range(heads):
            row = jnp.where(lane == shard * heads + h, ref[h], row)
            row = jnp.where(lane == HEADS + shard * heads + h, ref[h], row)
        par_send[6:7, place * LANES : (place + 1) * LANES] = row

    tail_load.wait()
    halo_pack[15:16, :] = jnp.zeros((1, 1024), F32)
    tail = tail_v[...].astype(F32)
    for r in range(KERNEL - 1):
        for c in range(CONV_DIM // 1024):
            halo_pack[r * 5 + c : r * 5 + c + 1, :] = tail[13 + r : 14 + r, c * 1024 : (c + 1) * 1024]
    halo_send[...] = halo_pack[...].astype(BF16)

    peers = shards - 1 + SIDE - 1 + high - 1
    at_end = jnp.logical_or(along_y == 0, along_y == SIDE - 1)

    @pl.when(at_end)
    def _():
        pl.semaphore_wait(barrier, peers + 1)

    @pl.when(jnp.logical_not(at_end))
    def _():
        pl.semaphore_wait(barrier, peers)


    def send_par(k, c):
        other, rise = peer(k)
        target = jnp.where(rise == 1, behind, me)
        remote(par_send, par.at[shard], par_sem.at[0], par_sem.at[1], {"fsdp": other, "seq": target}).start()
        return c

    def tell(offset, c):
        pl.semaphore_signal(ready, inc=1, device_id={"seq": shifted(me, offset, ranks)}, device_id_type=MESH)
        return c

    lax.fori_loop(1, shards, send_par, 0)
    halo_copy = remote(halo_send, halo_recv, halo_sem.at[0], halo_sem.at[1], {"seq": lax.rem(me + 1, ranks)})
    halo_copy.start()
    lax.fori_loop(1, SIDE, tell, 0)

    par[shard] = par_send[...]

    gate_load.wait()

    def gate_tile(o, c):
        at = pl.ds(pl.multiple_of(o * LANES, LANES), LANES)
        gates[o] = silu(gate_v[:, at].astype(F32)).astype(gates.dtype)
        return c

    lax.fori_loop(0, TILES, gate_tile, 0)
    conv_load.wait()
    step_load.wait()

    several = par.at[pl.ds(0, shards - 1)]
    pltpu.make_async_copy(several, several, par_sem.at[1]).wait()
    for j in range(shards // 2):
        left, right = par[2 * j], par[2 * j + 1]
        at = 5 * j * LANES
        wfull[:, at : at + 256] = left[:, 0:256]
        wfull[:, at + 256 : at + 384] = left[:, 256:384] + right[:, 0:128]
        wfull[:, at + 384 : at + 640] = right[:, 128:384]
    small = jnp.zeros((1, 3 * LANES), F32)
    for i in range(shards):
        gfull[:, i * 256 : (i + 1) * 256] = par[i, 5:6, 0:256]
        small = small + par[i, 6:7, :]
    decay_row, bias_row, skip_row = (small[:, i * LANES : (i + 1) * LANES] for i in range(3))

    halo_copy.wait()
    before = jnp.where(me == 0, 0.0, halo_recv[...].astype(F32))
    for r in range(KERNEL - 1):
        for c in range(CONV_DIM // 1024):
            halo[5 + r : 6 + r, c * 1024 : (c + 1) * 1024] = before[r * 5 + c : r * 5 + c + 1, :]

    def convolved(at):
        rows = jnp.concatenate([halo[:, at], conv_v[:, at].astype(F32)], axis=0)
        taps = wfull[:, at]
        total = taps[4:5] + taps[3:4] * rows[8:]
        for back in range(1, KERNEL):
            total = total + taps[3 - back : 4 - back] * pltpu.roll(rows, back, 0)[8:]
        return silu(total)

    step = step_v[...].astype(F32)
    step = jnp.concatenate([step, step], axis=0).T
    dt = jax.nn.softplus(step + bias_row)
    after = lax.broadcasted_iota(jnp.int32, (ROWS, ROWS), 0)
    ahead = lax.broadcasted_iota(jnp.int32, (ROWS, ROWS), 1)
    causal = after >= ahead
    lower = jnp.where(causal, 1.0, 0.0)
    rate2 = -jnp.exp(decay_row) * LOG2E
    cumul = jnp.dot(lower, dt * rate2, precision=lax.Precision.HIGHEST, preferred_element_type=F32)
    low_half = lax.broadcasted_iota(jnp.int32, (ROWS, LANES), 1) < HEADS

    def spread_parts(v):
        top, middle, low = three_parts(v)
        first = jnp.where(low_half[: v.shape[0]], top, middle)
        return first.astype(BF16), jnp.where(low_half[: v.shape[0]], low, 0.0).astype(BF16)

    cparts[:, 0:LANES], cparts[:, LANES:] = spread_parts(cumul)
    logdt[...] = jnp.log2(dt).T - cumul.T
    wide[0:ROWS, 0:LANES], wide[0:ROWS, LANES:] = spread_parts(dt * jnp.exp2(cumul[ROWS - 1 : ROWS] - cumul))
    wide[ROWS : 2 * ROWS, 0:LANES], wide[ROWS : 2 * ROWS, LANES:] = spread_parts(jnp.exp2(cumul))
    skip16 = jnp.broadcast_to(skip_row, (16, LANES))
    wide[2 * ROWS :, 0:LANES], wide[2 * ROWS :, LANES:] = spread_parts(skip16)

    for g in range(GROUPS):
        keys = convolved(slice(INNER + g * LANES, INNER + (g + 1) * LANES))
        keyt[g] = keys.T.astype(BF16)
        asked = convolved(slice(INNER + (GROUPS + g) * LANES, INNER + (GROUPS + g + 1) * LANES))
        query[g] = asked.astype(BF16)
        scores[g] = jnp.where(causal, dot(query[g], keyt[g]), 0.0)

    pick_row = lax.rem(lax.broadcasted_iota(jnp.int32, (2 * LANES, LANES), 0), HEADS)
    pick_half = lax.broadcasted_iota(jnp.int32, (2 * LANES, LANES), 1) // HEADS

    def local_state(o, state_ref, decay_out):
        at = pl.ds(pl.multiple_of(o * LANES, LANES), LANES)
        x = convolved(at)
        pick = jnp.where(pick_row == pick_half + 2 * o, 1.0, 0.0).astype(BF16)
        spread = dot(wide[...], pick)
        expc[o] = spread[ROWS : 2 * ROWS]
        xs[o] = x.astype(BF16)
        vals[o] = x * spread[2 * ROWS : 2 * ROWS + 1]
        weighted = (x * spread[0:ROWS]).astype(BF16)
        state_ref[...] = dot(keyt[lax.div(o, PER_GROUP)], weighted).astype(BF16)
        decay_out[...] = spread[2 * ROWS - 1 : 2 * ROWS]

    part = LANES // PIECES
    tall = part // CHUNKS

    def send_tiles(piece, targets, wanted, src, dst, send_sem, recv_sem):
        for c in range(CHUNKS):
            for target, want in zip(targets, wanted):

                @pl.when(want)
                def _():
                    rows = pl.ds(piece * part + c * tall, tall)
                    remote(src.at[target, rows], dst.at[me, rows], send_sem, recv_sem, {"seq": target}).start()

    def first_pass(offsets):
        targets = [shifted(me, offset, ranks) for offset in offsets]
        for target, offset in zip(targets, offsets):
            local_state(target, local_send.at[target], decay_send.at[target])

            @pl.when(offset != 0)
            def _():
                remote(decay_send.at[target], decay_recv.at[me], dec_sem.at[0], dec_sem.at[1], {"seq": target}).start()

            send_local(0, [target], [offset])

    last = ranks - 1

    def send_local(piece, targets, offsets):
        wanted = [jnp.logical_and(offset != 0, me != last) for offset in offsets]
        send_tiles(piece, targets, wanted, local_send, local_recv, loc_sem.at[PIECES], loc_sem.at[piece])

    pl.semaphore_wait(ready, SIDE - 1)
    for_groups(first_pass)
    for piece in range(1, PIECES):
        for_groups(lambda offsets: send_local(piece, [shifted(me, offset, ranks) for offset in offsets], offsets))
    local_recv[me] = local_send[me]
    decay_recv[me] = decay_send[me]

    ones_row = lax.rem(lax.broadcasted_iota(jnp.int32, (2 * LANES, 2 * LANES), 0), HEADS)
    ones_half = lax.broadcasted_iota(jnp.int32, (2 * LANES, 2 * LANES), 1) // LANES

    def inside(o, c):
        pick = jnp.where(ones_row == ones_half + 2 * o, 1.0, 0.0).astype(BF16)
        spread = dot(cparts[...], pick)
        score = scores[lax.div(o, PER_GROUP)]
        x = xs[o]
        zero = jnp.zeros_like(x)
        total = vals[o]
        for half in range(2):
            spot = spread[:, half * LANES : (half + 1) * LANES] + logdt[pl.ds(2 * o + half, 1), :]
            weights = jnp.exp2(jnp.minimum(spot, 64.0)) * score
            mine = jnp.where(low_half if half == 0 else jnp.logical_not(low_half), x, zero)
            total = total + dot(weights.astype(BF16), mine)
        vals[o] = total
        return c

    def wait_either(first, view, sem, one, other):
        for chosen, n in ((first, one), (jnp.logical_not(first), other)):
            if n:

                @pl.when(chosen)
                def _():
                    pltpu.make_async_copy(view(n), view(n), sem).wait()

    def send_states(piece):
        here = slice(piece * part, (piece + 1) * part)
        wait_either(me == last, lambda n: local_recv.at[pl.ds(0, n), here], loc_sem.at[piece], last, last - 1)

        def carry(s, state):
            state_send[s, here] = state.astype(BF16)
            return state * decay_recv[s] + local_recv[s, here].astype(F32)

        lax.fori_loop(0, ranks, carry, jnp.zeros((part, LANES), F32), unroll=4)

        def second_pass(offsets):
            targets = [shifted(me, offset, ranks) for offset in offsets]
            wanted = [jnp.logical_and(offset != 0, target != 0) for target, offset in zip(targets, offsets)]
            send_tiles(piece, targets, wanted, state_send, state_recv, st_send_sem, st_recv_sem.at[me])

        for_groups(second_pass)

    most_decay = decay_recv.at[pl.ds(0, ranks - 1)]
    lax.fori_loop(0, INSIDE_FIRST, inside, 0)
    pltpu.make_async_copy(most_decay, most_decay, dec_sem.at[1]).wait()
    send_states(0)
    lax.fori_loop(INSIDE_FIRST, TILES, inside, 0)
    for piece in range(1, PIECES):
        send_states(piece)
    state_recv[me] = state_send[me]
    square[...] = jnp.zeros_like(square)

    def arrive(offsets):
        for offset in offsets:
            o = shifted(me, offset, ranks, -1)

            @pl.when(jnp.logical_and(offset != 0, me != 0))
            def _():
                slot = state_recv.at[o]
                pltpu.make_async_copy(slot, slot, st_recv_sem.at[o]).wait()

            g = lax.div(o, PER_GROUP)
            value = (vals[o] + dot(query[g], state_recv[o]) * expc[o]) * gates[o].astype(F32)
            vals[o] = value
            square[g] = square[g] + value * value

    @pl.when(me == 0)
    def _():
        state_recv[...] = jnp.zeros_like(state_recv)

    for_groups(arrive)

    for g in range(GROUPS):
        mean = jnp.sum(square[g], axis=1, keepdims=True) * (1.0 / (PER_GROUP * LANES))
        inverse = lax.rsqrt(mean + EPS)
        for j in range(PER_GROUP):
            o = g * PER_GROUP + j
            out_ref[0, :, o * LANES : (o + 1) * LANES] = (
                vals[o] * inverse * gfull[:, o * LANES : (o + 1) * LANES]
            ).astype(BF16)

    pltpu.make_async_copy(several, several, par_sem.at[0]).wait()
    wait_either(me == last, lambda n: local_recv.at[pl.ds(0, n)], loc_sem.at[PIECES], 0, last)
    pltpu.make_async_copy(most_decay, most_decay, dec_sem.at[0]).wait()
    wait_either(me == 0, lambda n: state_send.at[pl.ds(0, n)], st_send_sem, last, last - 1)


def mixer(ranks, shards, *operands):
    tile = (TILES, ROWS, LANES)
    pair = (ranks, LANES, LANES)
    row = (ranks, 1, LANES)
    dma = pltpu.SemaphoreType.DMA
    far = pl.BlockSpec(memory_space=pl.ANY)
    return pl.pallas_call(
        functools.partial(kernel, ranks, shards),
        out_shape=pltpu.VMEM((1, ROWS, INNER), BF16),
        in_specs=[far] * 9,
        out_specs=pl.BlockSpec(memory_space=pltpu.VMEM),
        scratch_shapes=[
            pltpu.VMEM((KERNEL, CONV_DIM // shards), F32),
            pltpu.VMEM((CONV_DIM // shards,), F32),
            pltpu.SMEM((HEADS // shards,), F32),
            pltpu.SMEM((HEADS // shards,), F32),
            pltpu.SMEM((HEADS // shards,), F32),
            pltpu.VMEM((INNER // shards,), F32),
            pltpu.VMEM((ROWS, CONV_DIM), BF16),
            pltpu.VMEM((ROWS, INNER), BF16),
            pltpu.VMEM((HEADS, ROWS), BF16),
            pltpu.VMEM((16, CONV_DIM), BF16),
            pltpu.VMEM((16, 1024), F32),
            pltpu.VMEM((16, 1024), BF16),
            pltpu.VMEM((16, 1024), BF16),
            pltpu.VMEM((8, CONV_DIM), F32),
            pltpu.VMEM((8, 384), F32),
            pltpu.VMEM((shards, 8, 384), F32),
            pltpu.VMEM((8, CONV_DIM), F32),
            pltpu.VMEM((1, INNER), F32),
            pltpu.VMEM((2 * ROWS + 16, 2 * LANES), BF16),
            pltpu.VMEM((ROWS, 2 * LANES), BF16),
            pltpu.VMEM((LANES, ROWS), F32),
            pltpu.VMEM((GROUPS, LANES, ROWS), BF16),
            pltpu.VMEM((GROUPS, ROWS, LANES), BF16),
            pltpu.VMEM((GROUPS, ROWS, ROWS), F32),
            pltpu.VMEM(tile, BF16),
            pltpu.VMEM(tile, F32),
            pltpu.VMEM(tile, F32),
            pltpu.VMEM(tile, F32),
            pltpu.VMEM((GROUPS, ROWS, LANES), F32),
            pltpu.VMEM(pair, BF16),
            pltpu.VMEM(pair, BF16),
            pltpu.VMEM(row, F32),
            pltpu.VMEM(row, F32),
            pltpu.VMEM(pair, BF16),
            pltpu.VMEM(pair, BF16),
            dma((10,)),
            pltpu.SemaphoreType.REGULAR,
            dma((2,)),
            dma((2,)),
            dma((PIECES + 1,)),
            dma((2,)),
            dma,
            dma((ranks,)),
        ],
        compiler_params=pltpu.CompilerParams(
            collective_id=0, has_side_effects=True, vmem_limit_bytes=60 * 1024 * 1024
        ),
        name="mixer",
    )(*operands)


def solution(mesh):
    ranks, shards = mesh.shape["seq"], mesh.shape["fsdp"]

    def body(conv_input, gate_input, step_input, conv_weight, conv_bias, decay_log, step_bias, skip_weight, norm_gain):
        return mixer(
            ranks, shards, conv_input, gate_input, jnp.swapaxes(step_input, 1, 2),
            conv_weight, conv_bias, decay_log, step_bias, skip_weight, norm_gain,
        )

    return jax.shard_map(
        body,
        mesh=mesh,
        in_specs=(
            P("fsdp", "seq", None),
            P("fsdp", "seq", None),
            P("fsdp", "seq", None),
            P(None, "fsdp"),
            P("fsdp"),
            P("fsdp"),
            P("fsdp"),
            P("fsdp"),
            P("fsdp"),
        ),
        out_specs=P("fsdp", "seq", None),
        check_vma=False,
    )
```
